32 devices in a mesh: node: 8 (over y, x, core), state: 4 (over z).
Axes of the slice: x: 2, y: 2, z: 4, core: 2. Of those that a mesh axis runs over, the one named last changes fastest.
Arguments:
- states: float32 [6144, 3072], P('node', 'state'), may hold values from -0.078125 to 0.078125
- coeffs: float32 [3072, 512], P('state'), may hold values from -6 to 6
- cell_matrix: float32 [96, 125, 125], P('node'), may hold values from -0.5 to 0.5
- connect: int32 [96, 125], P('node'), may hold values from 0 to 831, as said below
- face_list: int32 [512], P('node'), may hold values from 0 to 767, as said below
- node_mass: float32 [6144], P('node'), may hold values from 0.25 to 4
Outputs:
- rotated: float32 [512, 6144], P('state', 'node')
- h_panel: float32 [512, 3072], P('node', 'state')
- m_panel: float32 [512, 3072], P('node', 'state')
The draws below stay inside these ranges and needn't reach their ends.
Inputs may be any that keep to these rules, and one draw needn't show every extreme that they name: `connect`: within each partition the cells cover a periodic in-plane slab of hexahedral elements of order 4; indices 768 and above name ghosts, every ghost and every owned node is used by some cell. `face_list`: the 64 entries of one partition are distinct.
All inputs are finite; a program needn't handle non-finite values.
Results may differ from the reference program's by a relative error of at most 0.000084.
Values sent between devices are 32-bit elements; how exact they have to be, the bound alone decides.
A program may use at most 64 MiB of HBM per device.

```python
import math
import jax
import jax.numpy as jnp
from jax import lax

ORDER = 4
NPE = 125
CXY = 2
CZC = 3
NXY = 8
LAYERS = 12
NODES_DEV = 768
FACE = 64
CELLS_DEV = 12
NODES = 6144
STATES = 3072
BLOCK = 512
N_NODE = 8


def node_labels(key):
    keys = jax.vmap(lambda index: jax.random.fold_in(key, index))(jnp.arange(N_NODE))
    return jax.vmap(lambda single: jax.random.permutation(single, NODES_DEV))(keys).astype(jnp.int32)


def grid_axis(position, count):
    extents = (CZC, CXY, CXY, ORDER + 1, ORDER + 1, ORDER + 1)
    shape = [1, 1, 1, 1, 1, 1]
    shape[position] = count
    values = jnp.arange(count, dtype=jnp.int32).reshape(shape)
    return jnp.broadcast_to(values, extents).reshape(-1)


def draw_connect(key, part):
    labels = node_labels(key)
    layer = ORDER * grid_axis(0, CZC) + grid_axis(3, ORDER + 1)
    column = (ORDER * grid_axis(1, CXY) + grid_axis(4, ORDER + 1)) % NXY
    across = (ORDER * grid_axis(2, CXY) + grid_axis(5, ORDER + 1)) % NXY
    planar = column * NXY + across
    canonical = jnp.minimum(layer * NXY * NXY + planar, NODES_DEV - 1).astype(jnp.int32)
    is_ghost = layer == LAYERS
    ghost_index = (NODES_DEV + planar).astype(jnp.int32)
    local = jnp.where(is_ghost[None, :], ghost_index[None, :], labels[:, canonical])
    return local.reshape(N_NODE * CELLS_DEV, NPE).astype(jnp.int32)


def draw_face_list(key, part):
    labels = node_labels(key)
    return labels[:, :FACE].reshape(N_NODE * FACE).astype(jnp.int32)


def steps_of(stream_key, shape, split, smallest, largest):
    def one(dim, blocks):
        draws = jax.random.uniform(jax.random.fold_in(jax.random.fold_in(stream_key, 6), dim), (blocks,), jnp.float32, smallest / len(split), largest / len(split))
        return jnp.repeat(jnp.exp(draws), shape[dim] // blocks).reshape((-1,) + (1,) * (len(shape) - dim - 1))

    level = one(*split[0])
    for cut in split[1:]:
        level = level * one(*cut)
    return level


def bell_draw(key, shape, spread, bound, shards=(), kind=jnp.bfloat16):
    drawn = spread * jax.random.normal(key, shape, jnp.float32)
    if shards:
        drawn = drawn * steps_of(key, shape, shards, -0.22, 0.18)
    return jnp.clip(drawn, -bound, bound).astype(kind)


def setup_inputs(seed: int = 0) -> dict:
    streams_of = jax.random.split(jax.random.key(seed), 7)
    return {
        "states": bell_draw(streams_of[0], (NODES, STATES), NODES ** -0.5, 0.078125, ((0, 8), (1, 4)), jnp.float32),
        "coeffs": bell_draw(streams_of[1], (STATES, BLOCK), 1.0, 6.0, ((0, 4),), jnp.float32),
        "cell_matrix": bell_draw(streams_of[2], (CELLS_DEV * N_NODE, NPE, NPE), NPE ** -0.5, 0.5, ((0, 8),), jnp.float32),
        "connect": draw_connect(jax.random.fold_in(streams_of[6], 71), 0),
        "face_list": draw_face_list(jax.random.fold_in(streams_of[6], 71), 0),
        "node_mass": jnp.clip(jnp.exp(math.log(4.0) - 2.7725887 * jax.random.uniform(streams_of[5], (NODES,), jnp.float32) ** steps_of(streams_of[5], (NODES,), ((0, 8),), -0.2, 0.2)), 0.25, 4.0),
    }


def apply_cells(block_rows, cell_matrix, connect, face_list):
    height = block_rows.shape[0]
    per_node = block_rows.reshape(height, N_NODE, NODES_DEV)
    face_sets = face_list.reshape(N_NODE, FACE)
    linkage = connect.reshape(N_NODE, CELLS_DEV, NPE)
    element = cell_matrix.reshape(N_NODE, CELLS_DEV, NPE, NPE)
    element = 0.5 * (element + jnp.swapaxes(element, 2, 3))
    face_values = jax.vmap(lambda values, picks: values[:, picks], in_axes=(1, 0), out_axes=1)(per_node, face_sets)
    ghosts = jnp.concatenate([face_values[:, 1:], jnp.zeros((height, 1, FACE), jnp.float32)], axis=1)
    extended = jnp.concatenate([per_node, ghosts], axis=2)

    def per_part(values, links, cells):
        cell_values = values[:, links]
        cell_output = jnp.einsum("cab,rcb->rca", cells, cell_values, precision=lax.Precision.HIGHEST)
        empty = jnp.zeros((height, NODES_DEV + FACE), jnp.float32)
        return empty.at[:, links.reshape(-1)].add(cell_output.reshape(height, -1))

    assembled = jax.vmap(per_part, in_axes=(1, 0, 0), out_axes=1)(extended, linkage, element)
    owned = assembled[:, :, :NODES_DEV]
    returned = jnp.concatenate([jnp.zeros((height, 1, FACE), jnp.float32), assembled[:, :-1, NODES_DEV:]], axis=1)
    owned = jax.vmap(lambda values, picks, extra: values.at[:, picks].add(extra), in_axes=(1, 0, 1), out_axes=1)(owned, face_sets, returned)
    return owned.reshape(height, NODES)


def reference(states, coeffs, cell_matrix, connect, face_list, node_mass):
    rotated = lax.dot_general(coeffs, states, (((0,), (1,)), ((), ())), precision=lax.Precision.HIGHEST, preferred_element_type=jnp.float32)
    applied = apply_cells(rotated, cell_matrix, connect, face_list)
    h_panel = jnp.dot(applied, states, precision=lax.Precision.HIGHEST, preferred_element_type=jnp.float32)
    m_panel = jnp.dot(rotated * node_mass[None, :], states, precision=lax.Precision.HIGHEST, preferred_element_type=jnp.float32)
    return rotated, h_panel, m_panel
```

```python
import functools

import jax
import jax.numpy as jnp
from jax import lax
from jax.experimental import pallas as pl
from jax.experimental.pallas import tpu as pltpu
from jax.sharding import PartitionSpec as P

MESH = pl.DeviceIdType.MESH
NN = (((1,), (0,)), ((), ()))
NT = (((1,), (1,)), ((), ()))
BF = jnp.bfloat16
F32 = jnp.float32


def split(x):
    hi = x.astype(BF)
    return hi, (x - hi.astype(F32)).astype(BF)


def mul(a, b, dims):
    return lax.dot_general(a, b, dims, preferred_element_type=F32)


def mul3(a, b, dims):
    return mul(a[0], b[0], dims) + (mul(a[0], b[1], dims) + mul(a[1], b[0], dims))


def kernel(
    n_node, n_state,
    states, coeffs, cells, links, faces, mass,
    rot, hout, mout,
    ct, xhi, xlo, part, rrecv, lrecv, rout, lout,
    st, thi, tlo, ahi, alo, wbuf, whi, wlo, ghost, gsend, wghost,
    qbuf, qrecv,
    rs_send, rs_recv, ls_send, ls_recv, q_send, q_recv, g_sem, w_sem,
):
    me = lax.axis_index("node")
    pos = lax.axis_index("state")
    nodes = states.shape[0]
    width = states.shape[1]
    ext = st.shape[0]
    count = cells.shape[0]
    face = ext - nodes
    chunks = qbuf.shape[0]
    pieces = part.shape[0]
    rows = n_node * 8
    last = n_state - 1

    def peer(k):
        return lax.rem(me + k, n_node)

    barrier = pltpu.get_barrier_semaphore()
    for k in range(1, n_node):
        pl.semaphore_signal(barrier, inc=1, device_id={"node": peer(k)}, device_id_type=MESH)

    @pl.when(pos > 0)
    def _():
        pl.semaphore_signal(barrier, inc=1, device_id={"state": pos - 1}, device_id_type=MESH)

    @pl.when(pos < last)
    def _():
        pl.semaphore_signal(barrier, inc=1, device_id={"state": pos + 1}, device_id_type=MESH)

    hi, lo = split(states[...])
    xhi[pl.ds(0, nodes)] = hi
    xlo[pl.ds(0, nodes)] = lo
    ct[...] = coeffs[...].T.reshape(ct.shape)

    @pl.when(pos == 0)
    def _():
        rrecv[...] = jnp.zeros_like(rrecv)

    @pl.when(pos == last)
    def _():
        lrecv[...] = jnp.zeros_like(lrecv)

    face_t = (lax.broadcasted_iota(jnp.int32, (nodes, 128), 0) == faces[...]).astype(F32)
    face_rows = face_t.T.astype(BF)
    picked = mul(face_rows, hi, NN) + mul(face_rows, lo, NN)
    gsend[...] = picked[:face]

    def rotate(t):
        a = split(ct[:, t].reshape(rows, width))
        value = mul3(a, (xhi[pl.ds(0, nodes)], xlo[pl.ds(0, nodes)]), NT)
        part[pl.ds(2 * t, 2)] = value.reshape(2, rows // 2, nodes)

    rotate(0)
    @pl.when((pos > 0) & (pos < last))
    def _():
        pl.semaphore_wait(barrier, n_node + 1)

    @pl.when((pos == 0) | (pos == last))
    def _():
        pl.semaphore_wait(barrier, n_node)

    def ghost_copy(to):
        return pltpu.make_async_remote_copy(
            src_ref=gsend, dst_ref=ghost, send_sem=g_sem.at[0], recv_sem=g_sem.at[1],
            device_id={"node": to}, device_id_type=MESH,
        )

    def back_copy(to):
        return pltpu.make_async_remote_copy(
            src_ref=wbuf.at[pl.ds(nodes, face)], dst_ref=wghost, send_sem=w_sem.at[0], recv_sem=w_sem.at[1],
            device_id={"node": to}, device_id_type=MESH,
        )

    def right_copy(q):
        return pltpu.make_async_remote_copy(
            src_ref=rout.at[q], dst_ref=rrecv.at[q], send_sem=rs_send.at[q], recv_sem=rs_recv.at[q],
            device_id={"state": lax.rem(pos + 1, n_state)}, device_id_type=MESH,
        )

    def left_copy(q):
        return pltpu.make_async_remote_copy(
            src_ref=lout.at[q], dst_ref=lrecv.at[q], send_sem=ls_send.at[q], recv_sem=ls_recv.at[q],
            device_id={"state": lax.rem(pos + last, n_state)}, device_id_type=MESH,
        )

    def panel_copy(t, k):
        return pltpu.make_async_remote_copy(
            src_ref=qbuf.at[t, peer(k)], dst_ref=qrecv.at[t, k - 1],
            send_sem=q_send.at[t, k - 1], recv_sem=q_recv.at[t, k - 1],
            device_id={"node": peer(k)}, device_id_type=MESH,
        )

    def line_step(h):
        q = h - 2 * pos

        @pl.when((q >= 0) & (q < pieces))
        def _():
            @pl.when(pos > 0)
            def _():
                right_copy(q).wait_recv()

            @pl.when(pos < last)
            def _():
                rout[q] = part[q] + rrecv[q]
                right_copy(q).start()

        g = h - 2 * (last - pos)

        @pl.when((g >= 0) & (g < pieces))
        def _():
            @pl.when(pos < last)
            def _():
                left_copy(g).wait_recv()

            @pl.when(pos > 0)
            def _():
                lout[g] = part[g] + lrecv[g]
                left_copy(g).start()

    def panel(t):
        both = pl.ds(2 * t, 2)
        total = part[both] + rrecv[both] + lrecv[both]
        total = total.reshape(rows, nodes)
        tiles = total.reshape(n_node, 8, nodes)
        owned = rot.shape[0]
        mine = jnp.zeros((owned, 8, nodes), F32)
        for z in range(n_state):
            mine = jnp.where(pos == z, tiles[z * owned:(z + 1) * owned], mine)
        rot[:, t] = mine
        h = mul3(split(total), (whi[...], wlo[...]), NN)
        qbuf[t, :, :, pl.ds(0, width)] = h.reshape(n_node, 8, width)
        m = mul3(split(total * mass[...]), (xhi[pl.ds(0, nodes)], xlo[pl.ds(0, nodes)]), NN)
        qbuf[t, :, :, pl.ds(width, width)] = m.reshape(n_node, 8, width)
        for k in range(1, n_node):
            panel_copy(t, k).start()

    def finish(t):
        value = qbuf[t, me]
        for k in range(1, n_node):
            panel_copy(t, k).wait_recv()
            value = value + qrecv[t, k - 1]
        hout[t] = value[:, :width]
        mout[t] = value[:, width:]

    line_step(0)

    @pl.when(me > 0)
    def _():
        ghost_copy(lax.rem(me + n_node - 1, n_node)).start()

    if chunks > 1:
        rotate(1)
    line_step(1)

    st[...] = (
        lax.broadcasted_iota(jnp.int32, st.shape, 0) == links[...]
    ).astype(F32).astype(BF)

    for c in range(count):
        cell = cells[c]
        cell = 0.5 * (cell + cell.T)
        chi, clo = split(cell)
        pick = st[:, 128 * c:128 * (c + 1)]
        t_hi, t_lo = split(mul(chi, pick, NT) + mul(clo, pick, NT))
        thi[pl.ds(128 * c, 128)] = t_hi
        tlo[pl.ds(128 * c, 128)] = t_lo
    line_step(2)
    if chunks > 2:
        rotate(2)
    a_hi, a_lo = split(mul(st[...], thi[...], NN) + mul(st[...], tlo[...], NN))
    ahi[...] = a_hi
    alo[...] = a_lo
    line_step(3)

    @pl.when(me < n_node - 1)
    def _():
        ghost_copy(lax.rem(me + 1, n_node)).wait_recv()

    @pl.when(me == n_node - 1)
    def _():
        ghost[...] = jnp.zeros_like(ghost)

    g_hi, g_lo = split(ghost[...])
    xhi[pl.ds(nodes, face)] = g_hi
    xlo[pl.ds(nodes, face)] = g_lo
    wbuf[...] = mul3((ahi[...], alo[...]), (xhi[...], xlo[...]), NN)

    @pl.when(me < n_node - 1)
    def _():
        back_copy(lax.rem(me + 1, n_node)).start()

    line_step(4)
    if chunks > 3:
        rotate(3)
    line_step(5)

    @pl.when(me > 0)
    def _():
        back_copy(lax.rem(me + n_node - 1, n_node)).wait_recv()

    @pl.when(me == 0)
    def _():
        wghost[...] = jnp.zeros_like(wghost)

    b_hi, b_lo = split(wghost[...])
    face_cols = face_t[:, :face].astype(BF)
    w_hi, w_lo = split(wbuf[pl.ds(0, nodes)] + mul(face_cols, b_hi, NN) + mul(face_cols, b_lo, NN))
    whi[...] = w_hi
    wlo[...] = w_lo

    def body(u, carry):
        line_step(2 * u)

        @pl.when(u + 1 < chunks)
        def _():
            rotate(u + 1)

        line_step(2 * u + 1)
        t = u - last

        @pl.when(t >= 0)
        def _():
            panel(t)

        @pl.when(t >= 2)
        def _():
            finish(t - 2)

        return carry

    lax.fori_loop(3, chunks + last, body, 0)
    for t in range(max(chunks - 2, 0), chunks):
        finish(t)

    @pl.when(me > 0)
    def _():
        ghost_copy(lax.rem(me + n_node - 1, n_node)).wait_send()

    @pl.when(me < n_node - 1)
    def _():
        back_copy(lax.rem(me + 1, n_node)).wait_send()

    @pl.loop(0, pieces)
    def _(q):
        @pl.when(pos < last)
        def _():
            right_copy(q).wait_send()

        @pl.when(pos > 0)
        def _():
            left_copy(q).wait_send()

    @pl.loop(0, chunks)
    def _(t):
        for k in range(1, n_node):
            panel_copy(t, k).wait_send()


def local(n_node, n_state, states, coeffs, cell_matrix, connect, face_list, node_mass):
    nodes, width = states.shape
    block = coeffs.shape[1]
    count, npe = connect.shape
    face = face_list.shape[0]
    ext = nodes + face
    chunks = block // n_node // 8
    half = n_node * 4
    pieces = 2 * chunks
    owned = n_node // n_state
    cells = jnp.pad(cell_matrix, ((0, 0), (0, 128 - npe), (0, 128 - npe)))
    links = jnp.pad(connect, ((0, 0), (0, 128 - npe)), constant_values=-1).reshape(1, count * 128)
    faces = jnp.pad(face_list, (0, 128 - face), constant_values=-1).reshape(1, 128)
    vmem = pl.BlockSpec(memory_space=pltpu.VMEM)
    line = pltpu.VMEM((pieces, half, nodes), F32)
    rot, h, m = pl.pallas_call(
        functools.partial(kernel, n_node, n_state),
        out_shape=(
            jax.ShapeDtypeStruct((owned, chunks, 8, nodes), F32),
            jax.ShapeDtypeStruct((chunks, 8, width), F32),
            jax.ShapeDtypeStruct((chunks, 8, width), F32),
        ),
        in_specs=[vmem] * 6,
        out_specs=(vmem,) * 3,
        scratch_shapes=[
            pltpu.VMEM((n_node, chunks, 8, width), F32),
            pltpu.VMEM((ext, width), BF),
            pltpu.VMEM((ext, width), BF),
            line, line, line, line, line,
            pltpu.VMEM((ext, count * 128), BF),
            pltpu.VMEM((count * 128, ext), BF),
            pltpu.VMEM((count * 128, ext), BF),
            pltpu.VMEM((ext, ext), BF),
            pltpu.VMEM((ext, ext), BF),
            pltpu.VMEM((ext, width), F32),
            pltpu.VMEM((nodes, width), BF),
            pltpu.VMEM((nodes, width), BF),
            pltpu.VMEM((face, width), F32),
            pltpu.VMEM((face, width), F32),
            pltpu.VMEM((face, width), F32),
            pltpu.VMEM((chunks, n_node, 8, 2 * width), F32),
            pltpu.VMEM((chunks, n_node - 1, 8, 2 * width), F32),
            pltpu.SemaphoreType.DMA((pieces,)),
            pltpu.SemaphoreType.DMA((pieces,)),
            pltpu.SemaphoreType.DMA((pieces,)),
            pltpu.SemaphoreType.DMA((pieces,)),
            pltpu.SemaphoreType.DMA((chunks, n_node - 1)),
            pltpu.SemaphoreType.DMA((chunks, n_node - 1)),
            pltpu.SemaphoreType.DMA((2,)),
            pltpu.SemaphoreType.DMA((2,)),
        ],
        compiler_params=pltpu.CompilerParams(
            collective_id=0, has_side_effects=True, vmem_limit_bytes=60 * 1024 * 1024
        ),
    )(states, coeffs, cells, links, faces, node_mass.reshape(1, nodes))
    return rot.reshape(block // n_state, nodes), h.reshape(block // n_node, width), m.reshape(block // n_node, width)


def solution(mesh):
    return jax.shard_map(
        functools.partial(local, mesh.shape["node"], mesh.shape["state"]),
        mesh=mesh,
        in_specs=(
            P("node", "state"),
            P("state", None),
            P("node", None, None),
            P("node", None),
            P("node"),
            P("node"),
        ),
        out_specs=(P("state", "node"), P("node", "state"), P("node", "state")),
        check_vma=False,
    )
```

```python
import functools

import jax
import jax.numpy as jnp
from jax import lax
from jax.experimental import pallas as pl
from jax.experimental.pallas import tpu as pltpu
from jax.sharding import PartitionSpec as P

MESH = pl.DeviceIdType.MESH
NN = (((1,), (0,)), ((), ()))
NT = (((1,), (1,)), ((), ()))
BF = jnp.bfloat16
F32 = jnp.float32


def split(x):
    hi = x.astype(BF)
    return hi, (x - hi.astype(F32)).astype(BF)


def mul(a, b, dims):
    return lax.dot_general(a, b, dims, preferred_element_type=F32)


def mul3(a, b, dims):
    return mul(a[0], b[0], dims) + (mul(a[0], b[1], dims) + mul(a[1], b[0], dims))


def kernel(
    n_node, n_state,
    states, coeffs, cell_matrix, connect, face_list, node_mass,
    rot, hout, mout,
    ct, xhi, xlo, part, rrecv, lrecv, rout, lout,
    cells, links, st, thi, tlo, ahi, alo, wbuf, whi, wlo, ghost, gsend, wghost,
    tot, qbuf, pairs, qsum, qrecv,
    rs_send, rs_recv, ls_send, ls_recv, p_send, p_recv, q_send, q_recv, g_sem, w_sem,
):
    me = lax.axis_index("node")
    pos = lax.axis_index("state")
    core = lax.rem(me, 2)
    chip = lax.div(me, 2)
    partner = me + 1 - 2 * core
    nodes, width = states.shape
    ext = st.shape[0]
    count, npe = connect.shape
    face = ext - nodes
    chunks = qbuf.shape[0]
    pieces = part.shape[0]
    rows = n_node * 8
    chips = n_node // 2
    last = n_state - 1
    steps = pieces + 2 * last
    owned = rot.shape[0]
    x = (xhi.at[pl.ds(0, nodes)], xlo.at[pl.ds(0, nodes)])

    barrier = pltpu.get_barrier_semaphore()
    for k in range(1, n_node):
        pl.semaphore_signal(
            barrier, inc=1, device_id={"node": lax.rem(me + k, n_node)}, device_id_type=MESH
        )

    @pl.when(pos > 0)
    def _():
        pl.semaphore_signal(barrier, inc=1, device_id={"state": pos - 1}, device_id_type=MESH)

    @pl.when(pos < last)
    def _():
        pl.semaphore_signal(barrier, inc=1, device_id={"state": pos + 1}, device_id_type=MESH)

    hi, lo = split(states[...])
    x[0][...] = hi
    x[1][...] = lo
    ct[...] = coeffs[...].T.reshape(ct.shape)

    def rotate(first, number):
        rows_of = [ct[:, t].reshape(rows, width) for t in range(first, first + number)]
        a = split(rows_of[0] if number == 1 else jnp.concatenate(rows_of, 0))
        value = mul3(a, (x[0][...], x[1][...]), NT)
        part[pl.ds(4 * first, 4 * number)] = value.reshape(4 * number, rows // 4, nodes)

    rotate(0, 1)

    @pl.when(pos == 0)
    def _():
        rrecv[...] = jnp.zeros_like(rrecv)

    @pl.when(pos == last)
    def _():
        lrecv[...] = jnp.zeros_like(lrecv)

    @pl.when((pos > 0) & (pos < last))
    def _():
        pl.semaphore_wait(barrier, n_node + 1)

    @pl.when((pos == 0) | (pos == last))
    def _():
        pl.semaphore_wait(barrier, n_node)

    def ghost_copy(to):
        return pltpu.make_async_remote_copy(
            src_ref=gsend, dst_ref=ghost, send_sem=g_sem.at[0], recv_sem=g_sem.at[1],
            device_id={"node": to}, device_id_type=MESH,
        )

    def back_copy(to):
        return pltpu.make_async_remote_copy(
            src_ref=wbuf.at[pl.ds(nodes, face)], dst_ref=wghost, send_sem=w_sem.at[0], recv_sem=w_sem.at[1],
            device_id={"node": to}, device_id_type=MESH,
        )

    def right_copy(q):
        return pltpu.make_async_remote_copy(
            src_ref=rout.at[q], dst_ref=rrecv.at[q], send_sem=rs_send.at[q], recv_sem=rs_recv.at[q],
            device_id={"state": lax.rem(pos + 1, n_state)}, device_id_type=MESH,
        )

    def left_copy(q):
        return pltpu.make_async_remote_copy(
            src_ref=lout.at[q], dst_ref=lrecv.at[q], send_sem=ls_send.at[q], recv_sem=ls_recv.at[q],
            device_id={"state": lax.rem(pos + last, n_state)}, device_id_type=MESH,
        )

    def pair_copy(t):
        return pltpu.make_async_remote_copy(
            src_ref=qbuf.at[t, :, 1 - core], dst_ref=pairs.at[t],
            send_sem=p_send.at[t], recv_sem=p_recv.at[t],
            device_id={"node": partner}, device_id_type=MESH,
        )

    def panel_copy(t, k):
        to = lax.rem(chip + k, chips)
        return pltpu.make_async_remote_copy(
            src_ref=qsum.at[t, to], dst_ref=qrecv.at[t, k - 1],
            send_sem=q_send.at[t, k - 1], recv_sem=q_recv.at[t, k - 1],
            device_id={"node": 2 * to + core}, device_id_type=MESH,
        )

    def line_step(h):
        q = h - 2 * pos

        @pl.when((q >= 0) & (q < pieces))
        def _():
            @pl.when(pos > 0)
            def _():
                right_copy(q).wait_recv()

            @pl.when(pos < last)
            def _():
                rout[q] = part[q] + rrecv[q]
                right_copy(q).start()

        g = h - 2 * (last - pos)

        @pl.when((g >= 0) & (g < pieces))
        def _():
            @pl.when(pos < last)
            def _():
                left_copy(g).wait_recv()

            @pl.when(pos > 0)
            def _():
                lout[g] = part[g] + lrecv[g]
                left_copy(g).start()

    def line_steps(begin, end):
        @pl.loop(begin, end)
        def _(h):
            line_step(h)

    line_step(0)
    face_t = (
        lax.broadcasted_iota(jnp.int32, (nodes, face), 0) == face_list[...].reshape(1, face)
    ).astype(F32)
    face_cols = face_t.astype(BF)
    face_rows = face_t.T.astype(BF)
    gsend[...] = mul(face_rows, x[0][...], NN) + mul(face_rows, x[1][...], NN)

    @pl.when(me > 0)
    def _():
        ghost_copy(lax.rem(me + n_node - 1, n_node)).start()

    line_step(1)
    rotate(1, 1)
    line_step(2)
    cells[...] = jnp.zeros_like(cells)
    cells[:, :npe, :npe] = cell_matrix[...]
    links[...] = jnp.full(links.shape, -1, jnp.int32)
    links[:count, :npe] = connect[...]
    for c in range(count):
        st[:, 128 * c:128 * (c + 1)] = (
            lax.broadcasted_iota(jnp.int32, (ext, 128), 0) == links[c:c + 1]
        ).astype(F32).astype(BF)
    line_step(3)
    if chunks > 2:
        rotate(2, 2)
    line_step(4)
    for c in range(count):
        cell = cells[c]
        chi, clo = split(0.5 * (cell + cell.T))
        pick = st[:, 128 * c:128 * (c + 1)]
        t_hi, t_lo = split(mul(chi, pick, NT) + mul(clo, pick, NT))
        thi[pl.ds(128 * c, 128)] = t_hi
        tlo[pl.ds(128 * c, 128)] = t_lo
        if c % 3 == 2:
            line_step(5 + c // 3)
    done = 5 + count // 3
    quarter = ext // 4
    for r in range(4):
        picks = st[pl.ds(quarter * r, quarter)]
        a_hi, a_lo = split(mul(picks, thi[...], NN) + mul(picks, tlo[...], NN))
        ahi[pl.ds(quarter * r, quarter)] = a_hi
        alo[pl.ds(quarter * r, quarter)] = a_lo
        line_step(done)
        done += 1

    @pl.when(me < n_node - 1)
    def _():
        ghost_copy(lax.rem(me + 1, n_node)).wait_recv()

    @pl.when(me == n_node - 1)
    def _():
        ghost[...] = jnp.zeros_like(ghost)

    g_hi, g_lo = split(ghost[...])
    xhi[pl.ds(nodes, face)] = g_hi
    xlo[pl.ds(nodes, face)] = g_lo

    def apply(begin, size):
        at = pl.ds(begin, size)
        wbuf[at] = mul3((ahi[at], alo[at]), (xhi[...], xlo[...]), NN)

    apply(nodes, face)

    @pl.when(me < n_node - 1)
    def _():
        back_copy(lax.rem(me + 1, n_node)).start()

    line_step(done)
    done += 1
    for t in range(4, chunks, 2):
        rotate(t, 2)
        line_step(done)
        done += 1
    third = nodes // 3
    for r in range(3):
        apply(third * r, third)
        line_step(done)
        done += 1

    @pl.when(me > 0)
    def _():
        back_copy(lax.rem(me + n_node - 1, n_node)).wait_recv()

    @pl.when(me == 0)
    def _():
        wghost[...] = jnp.zeros_like(wghost)

    b_hi, b_lo = split(wghost[...])
    w_hi, w_lo = split(wbuf[pl.ds(0, nodes)] + mul(face_cols, b_hi, NN) + mul(face_cols, b_lo, NN))
    whi[...] = w_hi
    wlo[...] = w_lo
    line_step(done)
    done += 1

    def ready(t):
        return jnp.minimum(jnp.maximum(done + 2 * t, 4 * t + 4 + 2 * last), steps)

    def finish(t):
        value = qsum[t, chip]
        for k in range(1, chips):
            panel_copy(t, k).wait_recv()
            value = value + qrecv[t, k - 1]
        hout[t] = value[:, :width]
        mout[t] = value[:, width:]

    line_steps(done, ready(0))

    def body(t, carry):
        begin, end = ready(t), ready(t + 1)
        middle = jnp.minimum(begin + 1, end)
        every = pl.ds(4 * t, 4)
        total = (part[every] + rrecv[every] + lrecv[every]).reshape(rows, nodes)
        tot[...] = total.reshape(n_node, 8, nodes)
        rot[:, t] = tot[pl.ds(pos * owned, owned)]
        h = mul3(split(total), (whi[...], wlo[...]), NN)
        qbuf[t, :, :, :, pl.ds(0, width)] = h.reshape(chips, 2, 8, width)
        line_steps(begin, middle)
        total = tot[...].reshape(rows, nodes)
        m = mul3(split(total * node_mass[...].reshape(1, nodes)), (x[0][...], x[1][...]), NN)
        qbuf[t, :, :, :, pl.ds(width, width)] = m.reshape(chips, 2, 8, width)
        pair_copy(t).start()
        line_steps(middle, end)
        pair_copy(t).wait_recv()
        qsum[t] = qbuf[t, :, core] + pairs[t]
        for k in range(1, chips):
            panel_copy(t, k).start()

        @pl.when(t > 0)
        def _():
            finish(t - 1)

        return carry

    lax.fori_loop(0, chunks, body, 0)
    finish(chunks - 1)

    @pl.when(me > 0)
    def _():
        ghost_copy(lax.rem(me + n_node - 1, n_node)).wait_send()

    @pl.when(me < n_node - 1)
    def _():
        back_copy(lax.rem(me + 1, n_node)).wait_send()

    @pl.loop(0, pieces)
    def _(q):
        @pl.when(pos < last)
        def _():
            right_copy(q).wait_send()

        @pl.when(pos > 0)
        def _():
            left_copy(q).wait_send()

    @pl.loop(0, chunks)
    def _(t):
        pair_copy(t).wait_send()
        for k in range(1, chips):
            panel_copy(t, k).wait_send()


def deliver(a, b, c, a_out, b_out, c_out, sems):
    copies = [
        pltpu.make_async_copy(source, target, sems.at[i])
        for i, (source, target) in enumerate(((a, a_out), (b, b_out), (c, c_out)))
    ]
    for copy in copies:
        copy.start()
    for copy in copies:
        copy.wait()


def local(n_node, n_state, states, coeffs, cell_matrix, connect, face_list, node_mass):
    nodes, width = states.shape
    block = coeffs.shape[1]
    count = connect.shape[0]
    face = face_list.shape[0]
    ext = nodes + face
    chunks = block // n_node // 8
    pieces = 4 * chunks
    chips = n_node // 2
    owned = n_node // n_state
    vmem = pl.BlockSpec(memory_space=pltpu.VMEM)
    line = pltpu.VMEM((pieces, n_node * 2, nodes), F32)
    outs = pl.pallas_call(
        functools.partial(kernel, n_node, n_state),
        out_shape=(
            jax.ShapeDtypeStruct((owned, chunks, 8, nodes), F32),
            jax.ShapeDtypeStruct((chunks, 8, width), F32),
            jax.ShapeDtypeStruct((chunks, 8, width), F32),
        ),
        in_specs=[vmem] * 6,
        out_specs=(vmem,) * 3,
        scratch_shapes=[
            pltpu.VMEM((n_node, chunks, 8, width), F32),
            pltpu.VMEM((ext, width), BF),
            pltpu.VMEM((ext, width), BF),
            line, line, line, line, line,
            pltpu.VMEM((count, 128, 128), F32),
            pltpu.VMEM((-(-count // 8) * 8, 128), jnp.int32),
            pltpu.VMEM((ext, count * 128), BF),
            pltpu.VMEM((count * 128, ext), BF),
            pltpu.VMEM((count * 128, ext), BF),
            pltpu.VMEM((ext, ext), BF),
            pltpu.VMEM((ext, ext), BF),
            pltpu.VMEM((ext, width), F32),
            pltpu.VMEM((nodes, width), BF),
            pltpu.VMEM((nodes, width), BF),
            pltpu.VMEM((face, width), F32),
            pltpu.VMEM((face, width), F32),
            pltpu.VMEM((face, width), F32),
            pltpu.VMEM((n_node, 8, nodes), F32),
            pltpu.VMEM((chunks, chips, 2, 8, 2 * width), F32),
            pltpu.VMEM((chunks, chips, 8, 2 * width), F32),
            pltpu.VMEM((chunks, chips, 8, 2 * width), F32),
            pltpu.VMEM((chunks, chips - 1, 8, 2 * width), F32),
            pltpu.SemaphoreType.DMA((pieces,)),
            pltpu.SemaphoreType.DMA((pieces,)),
            pltpu.SemaphoreType.DMA((pieces,)),
            pltpu.SemaphoreType.DMA((pieces,)),
            pltpu.SemaphoreType.DMA((chunks,)),
            pltpu.SemaphoreType.DMA((chunks,)),
            pltpu.SemaphoreType.DMA((chunks, chips - 1)),
            pltpu.SemaphoreType.DMA((chunks, chips - 1)),
            pltpu.SemaphoreType.DMA((2,)),
            pltpu.SemaphoreType.DMA((2,)),
        ],
        compiler_params=pltpu.CompilerParams(
            collective_id=0, has_side_effects=True, vmem_limit_bytes=60 * 1024 * 1024
        ),
    )(states, coeffs, cell_matrix, connect, face_list, node_mass)
    shapes = ((block // n_state, nodes), (block // n_node, width), (block // n_node, width))
    anywhere = pl.BlockSpec(memory_space=pl.ANY)
    return pl.pallas_call(
        deliver,
        out_shape=tuple(jax.ShapeDtypeStruct(shape, F32) for shape in shapes),
        in_specs=[anywhere] * 3,
        out_specs=(anywhere,) * 3,
        scratch_shapes=[pltpu.SemaphoreType.DMA((3,))],
        compiler_params=pltpu.CompilerParams(vmem_limit_bytes=60 * 1024 * 1024),
    )(*(out.reshape(shape) for out, shape in zip(outs, shapes)))


def solution(mesh):
    return jax.shard_map(
        functools.partial(local, mesh.shape["node"], mesh.shape["state"]),
        mesh=mesh,
        in_specs=(
            P("node", "state"),
            P("state", None),
            P("node", None, None),
            P("node", None),
            P("node"),
            P("node"),
        ),
        out_specs=(P("state", "node"), P("node", "state"), P("node", "state")),
        check_vma=False,
    )
```

```python
import functools

import jax
import jax.numpy as jnp
from jax import lax
from jax.experimental import pallas as pl
from jax.experimental.pallas import tpu as pltpu
from jax.sharding import PartitionSpec as P

MESH = pl.DeviceIdType.MESH
BF = jnp.bfloat16
F32 = jnp.float32


def split(x):
    hi = x.astype(BF)
    return hi, (x - hi.astype(F32)).astype(BF)


def mul(a, b):
    return jnp.dot(a, b, preferred_element_type=F32)


def mul3(a, b):
    return mul(a[0], b[0]) + (mul(a[0], b[1]) + mul(a[1], b[0]))


def mul3_stacked(a, b):
    rows = a.shape[0]
    hi, lo = split(a)
    both = mul(jnp.concatenate([hi, lo], 0), b[0])
    return both[:rows] + (both[rows:] + mul(hi, b[1]))


def kernel(
    n_node, n_state,
    states, coeffs, cell_matrix, connect, face_list, node_mass,
    rot, hout, mout,
    xhi, xlo, part, rrecv, lrecv, rout, lout,
    cells, links, st, twice, thi, tlo, ahi, alo, wbuf, whi, wlo, ghost, gsend, wghost,
    tot, qbuf, pairs, qsum, qrecv,
    rs_send, rs_recv, ls_send, ls_recv, p_send, p_recv, q_send, q_recv, g_sem, w_sem,
):
    me = lax.axis_index("node")
    pos = lax.axis_index("state")
    core = lax.rem(me, 2)
    chip = lax.div(me, 2)
    partner = me + 1 - 2 * core
    nodes, width = states.shape
    ext = st.shape[0]
    count, npe = connect.shape
    face = ext - nodes
    chunks, group, _ = hout.shape
    pieces = part.shape[0]
    per = pieces // chunks
    rows = n_node * group
    chips = n_node // 2
    last = n_state - 1
    steps = pieces + 2 * last
    owned = rot.shape[0]
    x = (xhi.at[pl.ds(0, nodes)], xlo.at[pl.ds(0, nodes)])

    barrier = pltpu.get_barrier_semaphore()
    for k in range(1, n_node):
        pl.semaphore_signal(
            barrier, inc=1, device_id={"node": lax.rem(me + k, n_node)}, device_id_type=MESH
        )

    @pl.when(pos > 0)
    def _():
        pl.semaphore_signal(barrier, inc=1, device_id={"state": pos - 1}, device_id_type=MESH)

    @pl.when(pos < last)
    def _():
        pl.semaphore_signal(barrier, inc=1, device_id={"state": pos + 1}, device_id_type=MESH)

    hi, lo = split(states[...])
    x[0][...] = hi
    x[1][...] = lo
    value = mul3((hi, lo), split(coeffs[...])).T
    value = value.reshape(n_node, chunks, group, nodes)
    owners = n_node // per
    for t in range(chunks):
        for j in range(per):
            part[per * t + j] = value[owners * j:owners * (j + 1), t].reshape(owners * group, nodes)

    @pl.when(pos == 0)
    def _():
        rrecv[...] = jnp.zeros_like(rrecv)

    @pl.when(pos == last)
    def _():
        lrecv[...] = jnp.zeros_like(lrecv)

    @pl.when((pos > 0) & (pos < last))
    def _():
        pl.semaphore_wait(barrier, n_node + 1)

    @pl.when((pos == 0) | (pos == last))
    def _():
        pl.semaphore_wait(barrier, n_node)

    def ghost_copy(to):
        return pltpu.make_async_remote_copy(
            src_ref=gsend, dst_ref=ghost, send_sem=g_sem.at[0], recv_sem=g_sem.at[1],
            device_id={"node": to}, device_id_type=MESH,
        )

    def back_copy(to):
        return pltpu.make_async_remote_copy(
            src_ref=wbuf.at[pl.ds(nodes, face)], dst_ref=wghost, send_sem=w_sem.at[0], recv_sem=w_sem.at[1],
            device_id={"node": to}, device_id_type=MESH,
        )

    def right_copy(q):
        return pltpu.make_async_remote_copy(
            src_ref=rout.at[q], dst_ref=rrecv.at[q], send_sem=rs_send.at[q], recv_sem=rs_recv.at[q],
            device_id={"state": lax.rem(pos + 1, n_state)}, device_id_type=MESH,
        )

    def left_copy(q):
        return pltpu.make_async_remote_copy(
            src_ref=lout.at[q], dst_ref=lrecv.at[q], send_sem=ls_send.at[q], recv_sem=ls_recv.at[q],
            device_id={"state": lax.rem(pos + last, n_state)}, device_id_type=MESH,
        )

    def pair_copy(e):
        return pltpu.make_async_remote_copy(
            src_ref=qbuf.at[e, :, 1 - core], dst_ref=pairs.at[e],
            send_sem=p_send.at[e], recv_sem=p_recv.at[e],
            device_id={"node": partner}, device_id_type=MESH,
        )

    def panel_copy(e, k):
        to = lax.rem(chip + k, chips)
        return pltpu.make_async_remote_copy(
            src_ref=qsum.at[e, to], dst_ref=qrecv.at[e, k - 1],
            send_sem=q_send.at[e, k - 1], recv_sem=q_recv.at[e, k - 1],
            device_id={"node": 2 * to + core}, device_id_type=MESH,
        )

    def line_step(h):
        q = h - 2 * pos

        @pl.when((q >= 0) & (q < pieces))
        def _():
            @pl.when(pos > 0)
            def _():
                right_copy(q).wait_recv()

            @pl.when(pos < last)
            def _():
                rout[q] = part[q] + rrecv[q]
                right_copy(q).start()

        g = h - 2 * (last - pos)

        @pl.when((g >= 0) & (g < pieces))
        def _():
            @pl.when(pos < last)
            def _():
                left_copy(g).wait_recv()

            @pl.when(pos > 0)
            def _():
                lout[g] = part[g] + lrecv[g]
                left_copy(g).start()

    def line_steps(begin, end):
        @pl.loop(begin, end)
        def _(h):
            line_step(h)

    line_step(0)
    face_t = (
        lax.broadcasted_iota(jnp.int32, (nodes, face), 0) == face_list[...].reshape(1, face)
    ).astype(F32)
    face_cols = face_t.astype(BF)
    face_rows = face_t.T.astype(BF)
    gsend[...] = mul(face_rows, x[0][...]) + mul(face_rows, x[1][...])

    @pl.when(me > 0)
    def _():
        ghost_copy(lax.rem(me + n_node - 1, n_node)).start()

    line_step(1)
    cells[...] = jnp.zeros_like(cells)
    cells[:, :npe, :npe] = cell_matrix[...]
    links[...] = jnp.full(links.shape, -1, jnp.int32)
    links[:count, :npe] = connect[...]
    columns = links[...].T
    done = 2
    for c in range(count):
        st[:, 128 * c:128 * (c + 1)] = (
            lax.broadcasted_iota(jnp.int32, (ext, 128), 0) == links[c:c + 1]
        ).astype(F32).astype(BF)
        pick = (
            lax.broadcasted_iota(jnp.int32, (128, ext), 1) == columns[:, c:c + 1]
        ).astype(F32).astype(BF)
        twice[pl.ds(0, 128)] = pick
        twice[pl.ds(128, 128)] = pick
        cell = cells[c]
        t_hi, t_lo = split(mul(jnp.concatenate(split(0.5 * (cell + cell.T)), 1), twice[...]))
        thi[pl.ds(128 * c, 128)] = t_hi
        tlo[pl.ds(128 * c, 128)] = t_lo
        if c % 4 == 3:
            line_step(done)
            done += 1
    for begin in range(0, ext - 128, 256):
        end = begin + 256 if ext - begin - 256 >= 128 else ext
        a_hi, a_lo = split(mul(st[...], thi[:, begin:end]) + mul(st[...], tlo[:, begin:end]))
        ahi[:, begin:end] = a_hi
        alo[:, begin:end] = a_lo
        line_step(done)
        done += 1

    @pl.when(me < n_node - 1)
    def _():
        ghost_copy(lax.rem(me + 1, n_node)).wait_recv()

    @pl.when(me == n_node - 1)
    def _():
        ghost[...] = jnp.zeros_like(ghost)

    g_hi, g_lo = split(ghost[...])
    xhi[pl.ds(nodes, face)] = g_hi
    xlo[pl.ds(nodes, face)] = g_lo

    at = pl.ds(nodes, face)
    wbuf[at] = mul3((ahi[at], alo[at]), (xhi[...], xlo[...]))

    @pl.when(me < n_node - 1)
    def _():
        back_copy(lax.rem(me + 1, n_node)).start()

    line_step(done)
    done += 1
    at = pl.ds(0, nodes)
    for begin in range(0, width, 256):
        cols = slice(begin, begin + 256)
        wbuf[at, cols] = mul3((ahi[at], alo[at]), (xhi[:, cols], xlo[:, cols]))
        line_step(done)
        done += 1

    @pl.when(me > 0)
    def _():
        back_copy(lax.rem(me + n_node - 1, n_node)).wait_recv()

    @pl.when(me == 0)
    def _():
        wghost[...] = jnp.zeros_like(wghost)

    b_hi, b_lo = split(wghost[...])
    w_hi, w_lo = split(wbuf[pl.ds(0, nodes)] + mul(face_cols, b_hi) + mul(face_cols, b_lo))
    whi[...] = w_hi
    wlo[...] = w_lo
    line_step(done)
    done += 1

    def ready(t):
        return jnp.minimum(jnp.maximum(done + 2 * t, per * (t + 1) + 2 * last), steps)

    def finish(t):
        for i, out in enumerate((hout, mout)):
            value = qsum[2 * t + i, chip]
            for k in range(1, chips):
                panel_copy(2 * t + i, k).wait_recv()
                value = value + qrecv[2 * t + i, k - 1]
            out[t] = value

    line_steps(done, ready(0))

    def body(t, carry):
        begin, end = ready(t), ready(t + 1)
        middle = jnp.minimum(begin + 1, end)
        every = pl.ds(per * t, per)
        total = (part[every] + rrecv[every] + lrecv[every]).reshape(rows, nodes)
        tot[...] = total.reshape(n_node, group, nodes)
        rot[:, t] = tot[pl.ds(pos * owned, owned)]
        qbuf[2 * t] = mul3_stacked(total, (whi[...], wlo[...])).reshape(chips, 2, group, width)
        pair_copy(2 * t).start()
        line_steps(begin, middle)
        total = tot[...].reshape(rows, nodes) * node_mass[...].reshape(1, nodes)
        qbuf[2 * t + 1] = mul3_stacked(total, (x[0][...], x[1][...])).reshape(chips, 2, group, width)
        pair_copy(2 * t + 1).start()
        for i in range(2):
            e = 2 * t + i
            pair_copy(e).wait_recv()
            qsum[e] = qbuf[e, :, core] + pairs[e]
            for k in range(1, chips):
                panel_copy(e, k).start()
            if i == 0:
                line_steps(middle, jnp.minimum(middle + 1, end))
        line_steps(jnp.minimum(middle + 1, end), end)

        @pl.when(t > 0)
        def _():
            finish(t - 1)

        return carry

    lax.fori_loop(0, chunks, body, 0)
    finish(chunks - 1)

    @pl.when(me > 0)
    def _():
        ghost_copy(lax.rem(me + n_node - 1, n_node)).wait_send()

    @pl.when(me < n_node - 1)
    def _():
        back_copy(lax.rem(me + 1, n_node)).wait_send()

    @pl.loop(0, pieces)
    def _(q):
        @pl.when(pos < last)
        def _():
            right_copy(q).wait_send()

        @pl.when(pos > 0)
        def _():
            left_copy(q).wait_send()

    @pl.loop(0, 2 * chunks)
    def _(e):
        pair_copy(e).wait_send()
        for k in range(1, chips):
            panel_copy(e, k).wait_send()


def deliver(a, b, c, a_out, b_out, c_out):
    a_out[...] = a[...]
    b_out[...] = b[...]
    c_out[...] = c[...]


def local(n_node, n_state, states, coeffs, cell_matrix, connect, face_list, node_mass):
    nodes, width = states.shape
    block = coeffs.shape[1]
    count = connect.shape[0]
    face = face_list.shape[0]
    ext = nodes + face
    group = 16
    chunks = block // n_node // group
    pieces = 4 * chunks
    chips = n_node // 2
    owned = n_node // n_state
    vmem = pl.BlockSpec(memory_space=pltpu.VMEM)
    line = pltpu.VMEM((pieces, n_node * group // 4, nodes), F32)
    outs = pl.pallas_call(
        functools.partial(kernel, n_node, n_state),
        out_shape=(
            jax.ShapeDtypeStruct((owned, chunks, group, nodes), F32),
            jax.ShapeDtypeStruct((chunks, group, width), F32),
            jax.ShapeDtypeStruct((chunks, group, width), F32),
        ),
        in_specs=[vmem] * 6,
        out_specs=(vmem,) * 3,
        scratch_shapes=[
            pltpu.VMEM((ext, width), BF),
            pltpu.VMEM((ext, width), BF),
            line, line, line, line, line,
            pltpu.VMEM((count, 128, 128), F32),
            pltpu.VMEM((-(-count // 8) * 8, 128), jnp.int32),
            pltpu.VMEM((ext, count * 128), BF),
            pltpu.VMEM((256, ext), BF),
            pltpu.VMEM((count * 128, ext), BF),
            pltpu.VMEM((count * 128, ext), BF),
            pltpu.VMEM((ext, ext), BF),
            pltpu.VMEM((ext, ext), BF),
            pltpu.VMEM((ext, width), F32),
            pltpu.VMEM((nodes, width), BF),
            pltpu.VMEM((nodes, width), BF),
            pltpu.VMEM((face, width), F32),
            pltpu.VMEM((face, width), F32),
            pltpu.VMEM((face, width), F32),
            pltpu.VMEM((n_node, group, nodes), F32),
            pltpu.VMEM((2 * chunks, chips, 2, group, width), F32),
            pltpu.VMEM((2 * chunks, chips, group, width), F32),
            pltpu.VMEM((2 * chunks, chips, group, width), F32),
            pltpu.VMEM((2 * chunks, chips - 1, group, width), F32),
            pltpu.SemaphoreType.DMA((pieces,)),
            pltpu.SemaphoreType.DMA((pieces,)),
            pltpu.SemaphoreType.DMA((pieces,)),
            pltpu.SemaphoreType.DMA((pieces,)),
            pltpu.SemaphoreType.DMA((2 * chunks,)),
            pltpu.SemaphoreType.DMA((2 * chunks,)),
            pltpu.SemaphoreType.DMA((2 * chunks, chips - 1)),
            pltpu.SemaphoreType.DMA((2 * chunks, chips - 1)),
            pltpu.SemaphoreType.DMA((2,)),
            pltpu.SemaphoreType.DMA((2,)),
        ],
        compiler_params=pltpu.CompilerParams(
            collective_id=0, has_side_effects=True, vmem_limit_bytes=60 * 1024 * 1024
        ),
    )(states, coeffs, cell_matrix, connect, face_list, node_mass)
    shapes = ((block // n_state, nodes), (block // n_node, width), (block // n_node, width))
    return pl.pallas_call(
        deliver,
        out_shape=tuple(jax.ShapeDtypeStruct(shape, F32) for shape in shapes),
        in_specs=[vmem] * 3,
        out_specs=(vmem,) * 3,
        compiler_params=pltpu.CompilerParams(vmem_limit_bytes=60 * 1024 * 1024),
    )(*(out.reshape(shape) for out, shape in zip(outs, shapes)))


def solution(mesh):
    return jax.shard_map(
        functools.partial(local, mesh.shape["node"], mesh.shape["state"]),
        mesh=mesh,
        in_specs=(
            P("node", "state"),
            P("state", None),
            P("node", None, None),
            P("node", None),
            P("node"),
            P("node"),
        ),
        out_specs=(P("state", "node"), P("node", "state"), P("node", "state")),
        check_vma=False,
    )
```

```python
import functools

import jax
import jax.numpy as jnp
from jax import lax
from jax.experimental import pallas as pl
from jax.experimental.pallas import tpu as pltpu
from jax.sharding import PartitionSpec as P

MESH = pl.DeviceIdType.MESH
BF = jnp.bfloat16
F32 = jnp.float32


def split(x):
    hi = x.astype(BF)
    return hi, (x - hi.astype(F32)).astype(BF)


def mul(a, b):
    return jnp.dot(a, b, preferred_element_type=F32)


def mul3(a, b):
    return mul(a[0], b[0]) + (mul(a[0], b[1]) + mul(a[1], b[0]))


def mul3_stacked(a, b):
    rows = a.shape[0]
    hi, lo = split(a)
    both = mul(jnp.concatenate([hi, lo], 0), b[0])
    return both[:rows] + (both[rows:] + mul(hi, b[1]))


def kernel(
    n_node, n_state,
    states, coeffs, cell_matrix, connect, face_list, node_mass,
    rot, hout, mout,
    xhi, xlo, part, rrecv, lrecv, rout, lout,
    cells, links, st, twice, thi, tlo, ahi, alo, wbuf, whi, wlo, ghost, gsend, wghost,
    tot, qbuf, pairs, qsum, qrecv,
    rs_send, rs_recv, ls_send, ls_recv, p_send, p_recv, q_send, q_recv, g_sem, w_sem,
):
    me = lax.axis_index("node")
    pos = lax.axis_index("state")
    core = lax.rem(me, 2)
    chip = lax.div(me, 2)
    partner = me + 1 - 2 * core
    nodes, width = states.shape
    ext = st.shape[0]
    count, npe = connect.shape
    face = ext - nodes
    chunks, group, _ = hout.shape
    pieces = part.shape[0]
    per = pieces // chunks
    rows = n_node * group
    chips = n_node // 2
    last = n_state - 1
    steps = pieces + 2 * last
    owned = rot.shape[0]
    x = (xhi.at[pl.ds(0, nodes)], xlo.at[pl.ds(0, nodes)])

    barrier = pltpu.get_barrier_semaphore()
    for k in range(1, n_node):
        pl.semaphore_signal(
            barrier, inc=1, device_id={"node": lax.rem(me + k, n_node)}, device_id_type=MESH
        )

    @pl.when(pos > 0)
    def _():
        pl.semaphore_signal(barrier, inc=1, device_id={"state": pos - 1}, device_id_type=MESH)

    @pl.when(pos < last)
    def _():
        pl.semaphore_signal(barrier, inc=1, device_id={"state": pos + 1}, device_id_type=MESH)

    hi, lo = split(states[...])
    x[0][...] = hi
    x[1][...] = lo
    value = mul3((hi, lo), split(coeffs[...])).T
    value = value.reshape(n_node, chunks, group, nodes)
    owners = n_node // per
    for t in range(chunks):
        for j in range(per):
            part[per * t + j] = value[owners * j:owners * (j + 1), t].reshape(owners * group, nodes)

    @pl.when(pos == 0)
    def _():
        rrecv[...] = jnp.zeros_like(rrecv)

    @pl.when(pos == last)
    def _():
        lrecv[...] = jnp.zeros_like(lrecv)

    @pl.when((pos > 0) & (pos < last))
    def _():
        pl.semaphore_wait(barrier, n_node + 1)

    @pl.when((pos == 0) | (pos == last))
    def _():
        pl.semaphore_wait(barrier, n_node)

    def ghost_copy(to):
        return pltpu.make_async_remote_copy(
            src_ref=gsend, dst_ref=ghost, send_sem=g_sem.at[0], recv_sem=g_sem.at[1],
            device_id={"node": to}, device_id_type=MESH,
        )

    def back_copy(to):
        return pltpu.make_async_remote_copy(
            src_ref=wbuf.at[pl.ds(nodes, face)], dst_ref=wghost, send_sem=w_sem.at[0], recv_sem=w_sem.at[1],
            device_id={"node": to}, device_id_type=MESH,
        )

    def right_copy(q):
        return pltpu.make_async_remote_copy(
            src_ref=rout.at[q], dst_ref=rrecv.at[q], send_sem=rs_send.at[q], recv_sem=rs_recv.at[q],
            device_id={"state": lax.rem(pos + 1, n_state)}, device_id_type=MESH,
        )

    def left_copy(q):
        return pltpu.make_async_remote_copy(
            src_ref=lout.at[q], dst_ref=lrecv.at[q], send_sem=ls_send.at[q], recv_sem=ls_recv.at[q],
            device_id={"state": lax.rem(pos + last, n_state)}, device_id_type=MESH,
        )

    def pair_copy(e):
        return pltpu.make_async_remote_copy(
            src_ref=qbuf.at[e, :, 1 - core], dst_ref=pairs.at[e],
            send_sem=p_send.at[e], recv_sem=p_recv.at[e],
            device_id={"node": partner}, device_id_type=MESH,
        )

    def panel_copy(e, k):
        to = lax.rem(chip + k, chips)
        return pltpu.make_async_remote_copy(
            src_ref=qsum.at[e, to], dst_ref=qrecv.at[e, k - 1],
            send_sem=q_send.at[e, k - 1], recv_sem=q_recv.at[e, k - 1],
            device_id={"node": 2 * to + core}, device_id_type=MESH,
        )

    def line_step(h):
        q = h - 2 * pos

        @pl.when((q >= 0) & (q < pieces))
        def _():
            @pl.when(pos > 0)
            def _():
                right_copy(q).wait_recv()

            @pl.when(pos < last)
            def _():
                rout[q] = part[q] + rrecv[q]
                right_copy(q).start()

        g = h - 2 * (last - pos)

        @pl.when((g >= 0) & (g < pieces))
        def _():
            @pl.when(pos < last)
            def _():
                left_copy(g).wait_recv()

            @pl.when(pos > 0)
            def _():
                lout[g] = part[g] + lrecv[g]
                left_copy(g).start()

    def line_steps(begin, end):
        @pl.loop(begin, end)
        def _(h):
            line_step(h)

    line_step(0)
    line_step(1)
    face_t = (
        lax.broadcasted_iota(jnp.int32, (nodes, face), 0) == face_list[...].reshape(1, face)
    ).astype(F32)
    face_cols = face_t.astype(BF)
    face_rows = face_t.T.astype(BF)
    gsend[...] = mul(face_rows, x[0][...]) + mul(face_rows, x[1][...])

    @pl.when(me > 0)
    def _():
        ghost_copy(lax.rem(me + n_node - 1, n_node)).start()

    line_step(2)
    cells[...] = jnp.zeros_like(cells)
    cells[:, :npe, :npe] = cell_matrix[...]
    links[...] = jnp.full(links.shape, -1, jnp.int32)
    links[:count, :npe] = connect[...]
    columns = links[...].T
    done = 3
    for c in range(count):
        st[:, 128 * c:128 * (c + 1)] = (
            lax.broadcasted_iota(jnp.int32, (ext, 128), 0) == links[c:c + 1]
        ).astype(F32).astype(BF)
        pick = (
            lax.broadcasted_iota(jnp.int32, (128, ext), 1) == columns[:, c:c + 1]
        ).astype(F32).astype(BF)
        twice[pl.ds(0, 128)] = pick
        twice[pl.ds(128, 128)] = pick
        cell = cells[c]
        t_hi, t_lo = split(mul(jnp.concatenate(split(0.5 * (cell + cell.T)), 1), twice[...]))
        thi[pl.ds(128 * c, 128)] = t_hi
        tlo[pl.ds(128 * c, 128)] = t_lo
        if c % 4 == 3:
            line_step(done)
            done += 1
    for begin in range(0, ext - 128, 256):
        end = begin + 256 if ext - begin - 256 >= 128 else ext
        a_hi, a_lo = split(mul(st[...], thi[:, begin:end]) + mul(st[...], tlo[:, begin:end]))
        ahi[:, begin:end] = a_hi
        alo[:, begin:end] = a_lo
        line_step(done)
        line_step(done + 1)
        done += 2

    @pl.when(me < n_node - 1)
    def _():
        ghost_copy(lax.rem(me + 1, n_node)).wait_recv()

    @pl.when(me == n_node - 1)
    def _():
        ghost[...] = jnp.zeros_like(ghost)

    g_hi, g_lo = split(ghost[...])
    xhi[pl.ds(nodes, face)] = g_hi
    xlo[pl.ds(nodes, face)] = g_lo

    at = pl.ds(nodes, face)
    wbuf[at] = mul3((ahi[at], alo[at]), (xhi[...], xlo[...]))

    @pl.when(me < n_node - 1)
    def _():
        back_copy(lax.rem(me + 1, n_node)).start()

    line_step(done)
    done += 1
    at = pl.ds(0, nodes)
    for begin in range(0, width, 256):
        cols = slice(begin, begin + 256)
        wbuf[at, cols] = mul3((ahi[at], alo[at]), (xhi[:, cols], xlo[:, cols]))
        line_step(done)
        line_step(done + 1)
        done += 2

    @pl.when(me > 0)
    def _():
        back_copy(lax.rem(me + n_node - 1, n_node)).wait_recv()

    @pl.when(me == 0)
    def _():
        wghost[...] = jnp.zeros_like(wghost)

    b_hi, b_lo = split(wghost[...])
    w_hi, w_lo = split(wbuf[pl.ds(0, nodes)] + mul(face_cols, b_hi) + mul(face_cols, b_lo))
    whi[...] = w_hi
    wlo[...] = w_lo
    line_step(done)
    done += 1

    def ready(t):
        return jnp.minimum(jnp.maximum(done + 2 * t, per * (t + 1) + 2 * last), steps)

    def finish(t):
        for i, out in enumerate((hout, mout)):
            value = qsum[2 * t + i, chip]
            for k in range(1, chips):
                panel_copy(2 * t + i, k).wait_recv()
                value = value + qrecv[2 * t + i, k - 1]
            out[t] = value

    def pass_on(e):
        pair_copy(e).wait_recv()
        qsum[e] = qbuf[e, :, core] + pairs[e]
        for k in range(1, chips):
            panel_copy(e, k).start()

    line_steps(done, ready(0))

    def body(t, carry):
        begin, end = ready(t), ready(t + 1)
        middle = jnp.minimum(begin + 1, end)
        every = pl.ds(per * t, per)
        total = (part[every] + rrecv[every] + lrecv[every]).reshape(rows, nodes)
        tot[...] = total.reshape(n_node, group, nodes)
        rot[:, t] = tot[pl.ds(pos * owned, owned)]
        qbuf[2 * t] = mul3_stacked(total, (whi[...], wlo[...])).reshape(chips, 2, group, width)
        pair_copy(2 * t).start()

        @pl.when(t > 0)
        def _():
            pass_on(2 * t - 1)

        line_steps(begin, middle)
        total = tot[...].reshape(rows, nodes) * node_mass[...].reshape(1, nodes)
        qbuf[2 * t + 1] = mul3_stacked(total, (x[0][...], x[1][...])).reshape(chips, 2, group, width)
        pair_copy(2 * t + 1).start()
        pass_on(2 * t)
        line_steps(middle, end)

        @pl.when(t > 1)
        def _():
            finish(t - 2)

        return carry

    lax.fori_loop(0, chunks, body, 0)
    pass_on(2 * chunks - 1)
    if chunks > 1:
        finish(chunks - 2)
    finish(chunks - 1)

    @pl.when(me > 0)
    def _():
        ghost_copy(lax.rem(me + n_node - 1, n_node)).wait_send()

    @pl.when(me < n_node - 1)
    def _():
        back_copy(lax.rem(me + 1, n_node)).wait_send()

    @pl.loop(0, pieces)
    def _(q):
        @pl.when(pos < last)
        def _():
            right_copy(q).wait_send()

        @pl.when(pos > 0)
        def _():
            left_copy(q).wait_send()

    @pl.loop(0, 2 * chunks)
    def _(e):
        pair_copy(e).wait_send()
        for k in range(1, chips):
            panel_copy(e, k).wait_send()


def deliver(a, b, c, a_out, b_out, c_out):
    a_out[...] = a[...]
    b_out[...] = b[...]
    c_out[...] = c[...]


def local(n_node, n_state, states, coeffs, cell_matrix, connect, face_list, node_mass):
    nodes, width = states.shape
    block = coeffs.shape[1]
    count = connect.shape[0]
    face = face_list.shape[0]
    ext = nodes + face
    group = 8
    chunks = block // n_node // group
    pieces = 4 * chunks
    chips = n_node // 2
    owned = n_node // n_state
    vmem = pl.BlockSpec(memory_space=pltpu.VMEM)
    line = pltpu.VMEM((pieces, n_node * group // 4, nodes), F32)
    outs = pl.pallas_call(
        functools.partial(kernel, n_node, n_state),
        out_shape=(
            jax.ShapeDtypeStruct((owned, chunks, group, nodes), F32),
            jax.ShapeDtypeStruct((chunks, group, width), F32),
            jax.ShapeDtypeStruct((chunks, group, width), F32),
        ),
        in_specs=[vmem] * 6,
        out_specs=(vmem,) * 3,
        scratch_shapes=[
            pltpu.VMEM((ext, width), BF),
            pltpu.VMEM((ext, width), BF),
            line, line, line, line, line,
            pltpu.VMEM((count, 128, 128), F32),
            pltpu.VMEM((-(-count // 8) * 8, 128), jnp.int32),
            pltpu.VMEM((ext, count * 128), BF),
            pltpu.VMEM((256, ext), BF),
            pltpu.VMEM((count * 128, ext), BF),
            pltpu.VMEM((count * 128, ext), BF),
            pltpu.VMEM((ext, ext), BF),
            pltpu.VMEM((ext, ext), BF),
            pltpu.VMEM((ext, width), F32),
            pltpu.VMEM((nodes, width), BF),
            pltpu.VMEM((nodes, width), BF),
            pltpu.VMEM((face, width), F32),
            pltpu.VMEM((face, width), F32),
            pltpu.VMEM((face, width), F32),
            pltpu.VMEM((n_node, group, nodes), F32),
            pltpu.VMEM((2 * chunks, chips, 2, group, width), F32),
            pltpu.VMEM((2 * chunks, chips, group, width), F32),
            pltpu.VMEM((2 * chunks, chips, group, width), F32),
            pltpu.VMEM((2 * chunks, chips - 1, group, width), F32),
            pltpu.SemaphoreType.DMA((pieces,)),
            pltpu.SemaphoreType.DMA((pieces,)),
            pltpu.SemaphoreType.DMA((pieces,)),
            pltpu.SemaphoreType.DMA((pieces,)),
            pltpu.SemaphoreType.DMA((2 * chunks,)),
            pltpu.SemaphoreType.DMA((2 * chunks,)),
            pltpu.SemaphoreType.DMA((2 * chunks, chips - 1)),
            pltpu.SemaphoreType.DMA((2 * chunks, chips - 1)),
            pltpu.SemaphoreType.DMA((2,)),
            pltpu.SemaphoreType.DMA((2,)),
        ],
        compiler_params=pltpu.CompilerParams(
            collective_id=0, has_side_effects=True, vmem_limit_bytes=60 * 1024 * 1024
        ),
    )(states, coeffs, cell_matrix, connect, face_list, node_mass)
    shapes = ((block // n_state, nodes), (block // n_node, width), (block // n_node, width))
    return pl.pallas_call(
        deliver,
        out_shape=tuple(jax.ShapeDtypeStruct(shape, F32) for shape in shapes),
        in_specs=[vmem] * 3,
        out_specs=(vmem,) * 3,
        compiler_params=pltpu.CompilerParams(vmem_limit_bytes=60 * 1024 * 1024),
    )(*(out.reshape(shape) for out, shape in zip(outs, shapes)))


def solution(mesh):
    return jax.shard_map(
        functools.partial(local, mesh.shape["node"], mesh.shape["state"]),
        mesh=mesh,
        in_specs=(
            P("node", "state"),
            P("state", None),
            P("node", None, None),
            P("node", None),
            P("node"),
            P("node"),
        ),
        out_specs=(P("state", "node"), P("node", "state"), P("node", "state")),
        check_vma=False,
    )
```

```python
import functools

import jax
import jax.numpy as jnp
from jax import lax
from jax.experimental import pallas as pl
from jax.experimental.pallas import tpu as pltpu
from jax.sharding import PartitionSpec as P

MESH = pl.DeviceIdType.MESH
BF = jnp.bfloat16
F32 = jnp.float32


def split(x):
    hi = x.astype(BF)
    return hi, (x - hi.astype(F32)).astype(BF)


def mul(a, b):
    return jnp.dot(a, b, preferred_element_type=F32)


def mul3(a, b):
    return mul(a[0], b[0]) + (mul(a[0], b[1]) + mul(a[1], b[0]))


def mul3_stacked(a, b):
    rows = a.shape[0]
    hi, lo = split(a)
    both = mul(jnp.concatenate([hi, lo], 0), b[0])
    return both[:rows] + (both[rows:] + mul(hi, b[1]))


def kernel(
    n_node, n_state,
    states, coeffs, cell_matrix, connect, face_list, node_mass,
    rot, hout, mout,
    xhi, xlo, part, rrecv, lrecv, rout, lout,
    cells, links, st, twice, thi, tlo, ahi, alo, wbuf, whi, wlo, ghost, gsend, wghost,
    tot, qbuf, pairs, qsum, qrecv,
    rs_send, rs_recv, ls_send, ls_recv, p_send, p_recv, q_send, q_recv, g_sem, w_sem,
):
    me = lax.axis_index("node")
    pos = lax.axis_index("state")
    core = lax.rem(me, 2)
    chip = lax.div(me, 2)
    partner = me + 1 - 2 * core
    nodes, width = states.shape
    ext = st.shape[0]
    count, npe = connect.shape
    face = ext - nodes
    chunks, group, _ = hout.shape
    pieces = part.shape[0]
    per = pieces // chunks
    rows = n_node * group
    chips = n_node // 2
    last = n_state - 1
    lag = 3
    steps = pieces + lag * last
    owned = rot.shape[0]
    x = (xhi.at[pl.ds(0, nodes)], xlo.at[pl.ds(0, nodes)])

    barrier = pltpu.get_barrier_semaphore()
    for k in range(1, n_node):
        pl.semaphore_signal(
            barrier, inc=1, device_id={"node": lax.rem(me + k, n_node)}, device_id_type=MESH
        )

    @pl.when(pos > 0)
    def _():
        pl.semaphore_signal(barrier, inc=1, device_id={"state": pos - 1}, device_id_type=MESH)

    @pl.when(pos < last)
    def _():
        pl.semaphore_signal(barrier, inc=1, device_id={"state": pos + 1}, device_id_type=MESH)

    hi, lo = split(states[...])
    x[0][...] = hi
    x[1][...] = lo
    value = mul3((hi, lo), split(coeffs[...])).T
    value = value.reshape(n_node, chunks, group, nodes)
    owners = n_node // per
    for t in range(chunks):
        for j in range(per):
            part[per * t + j] = value[owners * j:owners * (j + 1), t].reshape(owners * group, nodes)

    @pl.when(pos == 0)
    def _():
        rrecv[...] = jnp.zeros_like(rrecv)

    @pl.when(pos == last)
    def _():
        lrecv[...] = jnp.zeros_like(lrecv)

    @pl.when((pos > 0) & (pos < last))
    def _():
        pl.semaphore_wait(barrier, n_node + 1)

    @pl.when((pos == 0) | (pos == last))
    def _():
        pl.semaphore_wait(barrier, n_node)

    def ghost_copy(to):
        return pltpu.make_async_remote_copy(
            src_ref=gsend, dst_ref=ghost, send_sem=g_sem.at[0], recv_sem=g_sem.at[1],
            device_id={"node": to}, device_id_type=MESH,
        )

    def back_copy(to):
        return pltpu.make_async_remote_copy(
            src_ref=wbuf.at[pl.ds(nodes, face)], dst_ref=wghost, send_sem=w_sem.at[0], recv_sem=w_sem.at[1],
            device_id={"node": to}, device_id_type=MESH,
        )

    def right_copy(q):
        return pltpu.make_async_remote_copy(
            src_ref=rout.at[q], dst_ref=rrecv.at[q], send_sem=rs_send.at[q], recv_sem=rs_recv.at[q],
            device_id={"state": lax.rem(pos + 1, n_state)}, device_id_type=MESH,
        )

    def left_copy(q):
        return pltpu.make_async_remote_copy(
            src_ref=lout.at[q], dst_ref=lrecv.at[q], send_sem=ls_send.at[q], recv_sem=ls_recv.at[q],
            device_id={"state": lax.rem(pos + last, n_state)}, device_id_type=MESH,
        )

    def pair_copy(e):
        return pltpu.make_async_remote_copy(
            src_ref=qbuf.at[e, :, 1 - core], dst_ref=pairs.at[e],
            send_sem=p_send.at[e], recv_sem=p_recv.at[e],
            device_id={"node": partner}, device_id_type=MESH,
        )

    def panel_copy(e, k):
        to = lax.rem(chip + k, chips)
        return pltpu.make_async_remote_copy(
            src_ref=qsum.at[e, to], dst_ref=qrecv.at[e, k - 1],
            send_sem=q_send.at[e, k - 1], recv_sem=q_recv.at[e, k - 1],
            device_id={"node": 2 * to + core}, device_id_type=MESH,
        )

    def line_step(h):
        q = h - lag * pos

        @pl.when((q >= 0) & (q < pieces))
        def _():
            @pl.when(pos > 0)
            def _():
                right_copy(q).wait_recv()

            @pl.when(pos < last)
            def _():
                rout[q] = part[q] + rrecv[q]
                right_copy(q).start()

        g = h - lag * (last - pos)

        @pl.when((g >= 0) & (g < pieces))
        def _():
            @pl.when(pos < last)
            def _():
                left_copy(g).wait_recv()

            @pl.when(pos > 0)
            def _():
                lout[g] = part[g] + lrecv[g]
                left_copy(g).start()

    def line_steps(begin, end):
        @pl.loop(begin, end)
        def _(h):
            line_step(h)

    for done in range(lag):
        line_step(done)
    face_t = (
        lax.broadcasted_iota(jnp.int32, (nodes, face), 0) == face_list[...].reshape(1, face)
    ).astype(F32)
    face_cols = face_t.astype(BF)
    face_rows = face_t.T.astype(BF)
    gsend[...] = mul(face_rows, x[0][...]) + mul(face_rows, x[1][...])

    @pl.when(me > 0)
    def _():
        ghost_copy(lax.rem(me + n_node - 1, n_node)).start()

    line_step(lag)
    cells[...] = jnp.zeros_like(cells)
    cells[:, :npe, :npe] = cell_matrix[...]
    links[...] = jnp.full(links.shape, -1, jnp.int32)
    links[:count, :npe] = connect[...]
    columns = links[...].T
    done = lag + 1
    for c in range(count):
        st[:, 128 * c:128 * (c + 1)] = (
            lax.broadcasted_iota(jnp.int32, (ext, 128), 0) == links[c:c + 1]
        ).astype(F32).astype(BF)
        pick = (
            lax.broadcasted_iota(jnp.int32, (128, ext), 1) == columns[:, c:c + 1]
        ).astype(F32).astype(BF)
        twice[pl.ds(0, 128)] = pick
        twice[pl.ds(128, 128)] = pick
        cell = cells[c]
        t_hi, t_lo = split(mul(jnp.concatenate(split(0.5 * (cell + cell.T)), 1), twice[...]))
        thi[pl.ds(128 * c, 128)] = t_hi
        tlo[pl.ds(128 * c, 128)] = t_lo
        if c % 4 == 3:
            line_step(done)
            done += 1
    for begin in range(0, ext - 128, 256):
        end = begin + 256 if ext - begin - 256 >= 128 else ext
        a_hi, a_lo = split(mul(st[...], thi[:, begin:end]) + mul(st[...], tlo[:, begin:end]))
        ahi[:, begin:end] = a_hi
        alo[:, begin:end] = a_lo
        line_step(done)
        done += 1

    @pl.when(me < n_node - 1)
    def _():
        ghost_copy(lax.rem(me + 1, n_node)).wait_recv()

    @pl.when(me == n_node - 1)
    def _():
        ghost[...] = jnp.zeros_like(ghost)

    g_hi, g_lo = split(ghost[...])
    xhi[pl.ds(nodes, face)] = g_hi
    xlo[pl.ds(nodes, face)] = g_lo

    at = pl.ds(nodes, face)
    wbuf[at] = mul3((ahi[at], alo[at]), (xhi[...], xlo[...]))

    @pl.when(me < n_node - 1)
    def _():
        back_copy(lax.rem(me + 1, n_node)).start()

    line_step(done)
    done += 1
    at = pl.ds(0, nodes)
    for begin in range(0, width, 256):
        cols = slice(begin, begin + 256)
        wbuf[at, cols] = mul3((ahi[at], alo[at]), (xhi[:, cols], xlo[:, cols]))
        line_step(done)
        done += 1

    @pl.when(me > 0)
    def _():
        back_copy(lax.rem(me + n_node - 1, n_node)).wait_recv()

    @pl.when(me == 0)
    def _():
        wghost[...] = jnp.zeros_like(wghost)

    b_hi, b_lo = split(wghost[...])
    w_hi, w_lo = split(wbuf[pl.ds(0, nodes)] + mul(face_cols, b_hi) + mul(face_cols, b_lo))
    whi[...] = w_hi
    wlo[...] = w_lo
    line_step(done)
    done += 1

    def ready(t):
        return jnp.minimum(jnp.maximum(done + 2 * t, per * (t + 1) + lag * last), steps)

    def finish(t):
        for i, out in enumerate((hout, mout)):
            value = qsum[2 * t + i, chip]
            for k in range(1, chips):
                panel_copy(2 * t + i, k).wait_recv()
                value = value + qrecv[2 * t + i, k - 1]
            out[t] = value

    def pass_on(e):
        pair_copy(e).wait_recv()
        qsum[e] = qbuf[e, :, core] + pairs[e]
        for k in range(1, chips):
            panel_copy(e, k).start()

    line_steps(done, ready(0))

    def body(t, carry):
        begin, end = ready(t), ready(t + 1)
        middle = jnp.minimum(begin + 1, end)
        every = pl.ds(per * t, per)
        total = (part[every] + rrecv[every] + lrecv[every]).reshape(rows, nodes)
        tot[...] = total.reshape(n_node, group, nodes)
        rot[:, t] = tot[pl.ds(pos * owned, owned)]
        qbuf[2 * t] = mul3_stacked(total, (whi[...], wlo[...])).reshape(chips, 2, group, width)
        pair_copy(2 * t).start()

        @pl.when(t > 0)
        def _():
            pass_on(2 * t - 1)

        line_steps(begin, middle)
        total = tot[...].reshape(rows, nodes) * node_mass[...].reshape(1, nodes)
        qbuf[2 * t + 1] = mul3_stacked(total, (x[0][...], x[1][...])).reshape(chips, 2, group, width)
        pair_copy(2 * t + 1).start()
        pass_on(2 * t)
        line_steps(middle, end)

        @pl.when(t > 1)
        def _():
            finish(t - 2)

        return carry

    lax.fori_loop(0, chunks, body, 0)
    pass_on(2 * chunks - 1)
    if chunks > 1:
        finish(chunks - 2)
    finish(chunks - 1)

    @pl.when(me > 0)
    def _():
        ghost_copy(lax.rem(me + n_node - 1, n_node)).wait_send()

    @pl.when(me < n_node - 1)
    def _():
        back_copy(lax.rem(me + 1, n_node)).wait_send()

    @pl.loop(0, pieces)
    def _(q):
        @pl.when(pos < last)
        def _():
            right_copy(q).wait_send()

        @pl.when(pos > 0)
        def _():
            left_copy(q).wait_send()

    @pl.loop(0, 2 * chunks)
    def _(e):
        pair_copy(e).wait_send()
        for k in range(1, chips):
            panel_copy(e, k).wait_send()


def deliver(a, b, c, a_out, b_out, c_out):
    a_out[...] = a[...]
    b_out[...] = b[...]
    c_out[...] = c[...]


def local(n_node, n_state, states, coeffs, cell_matrix, connect, face_list, node_mass):
    nodes, width = states.shape
    block = coeffs.shape[1]
    count = connect.shape[0]
    face = face_list.shape[0]
    ext = nodes + face
    group = 16
    chunks = block // n_node // group
    pieces = 4 * chunks
    chips = n_node // 2
    owned = n_node // n_state
    vmem = pl.BlockSpec(memory_space=pltpu.VMEM)
    line = pltpu.VMEM((pieces, n_node * group // 4, nodes), F32)
    outs = pl.pallas_call(
        functools.partial(kernel, n_node, n_state),
        out_shape=(
            jax.ShapeDtypeStruct((owned, chunks, group, nodes), F32),
            jax.ShapeDtypeStruct((chunks, group, width), F32),
            jax.ShapeDtypeStruct((chunks, group, width), F32),
        ),
        in_specs=[vmem] * 6,
        out_specs=(vmem,) * 3,
        scratch_shapes=[
            pltpu.VMEM((ext, width), BF),
            pltpu.VMEM((ext, width), BF),
            line, line, line, line, line,
            pltpu.VMEM((count, 128, 128), F32),
            pltpu.VMEM((-(-count // 8) * 8, 128), jnp.int32),
            pltpu.VMEM((ext, count * 128), BF),
            pltpu.VMEM((256, ext), BF),
            pltpu.VMEM((count * 128, ext), BF),
            pltpu.VMEM((count * 128, ext), BF),
            pltpu.VMEM((ext, ext), BF),
            pltpu.VMEM((ext, ext), BF),
            pltpu.VMEM((ext, width), F32),
            pltpu.VMEM((nodes, width), BF),
            pltpu.VMEM((nodes, width), BF),
            pltpu.VMEM((face, width), F32),
            pltpu.VMEM((face, width), F32),
            pltpu.VMEM((face, width), F32),
            pltpu.VMEM((n_node, group, nodes), F32),
            pltpu.VMEM((2 * chunks, chips, 2, group, width), F32),
            pltpu.VMEM((2 * chunks, chips, group, width), F32),
            pltpu.VMEM((2 * chunks, chips, group, width), F32),
            pltpu.VMEM((2 * chunks, chips - 1, group, width), F32),
            pltpu.SemaphoreType.DMA((pieces,)),
            pltpu.SemaphoreType.DMA((pieces,)),
            pltpu.SemaphoreType.DMA((pieces,)),
            pltpu.SemaphoreType.DMA((pieces,)),
            pltpu.SemaphoreType.DMA((2 * chunks,)),
            pltpu.SemaphoreType.DMA((2 * chunks,)),
            pltpu.SemaphoreType.DMA((2 * chunks, chips - 1)),
            pltpu.SemaphoreType.DMA((2 * chunks, chips - 1)),
            pltpu.SemaphoreType.DMA((2,)),
            pltpu.SemaphoreType.DMA((2,)),
        ],
        compiler_params=pltpu.CompilerParams(
            collective_id=0, has_side_effects=True, vmem_limit_bytes=60 * 1024 * 1024
        ),
    )(states, coeffs, cell_matrix, connect, face_list, node_mass)
    shapes = ((block // n_state, nodes), (block // n_node, width), (block // n_node, width))
    return pl.pallas_call(
        deliver,
        out_shape=tuple(jax.ShapeDtypeStruct(shape, F32) for shape in shapes),
        in_specs=[vmem] * 3,
        out_specs=(vmem,) * 3,
        compiler_params=pltpu.CompilerParams(vmem_limit_bytes=60 * 1024 * 1024),
    )(*(out.reshape(shape) for out, shape in zip(outs, shapes)))


def solution(mesh):
    return jax.shard_map(
        functools.partial(local, mesh.shape["node"], mesh.shape["state"]),
        mesh=mesh,
        in_specs=(
            P("node", "state"),
            P("state", None),
            P("node", None, None),
            P("node", None),
            P("node"),
            P("node"),
        ),
        out_specs=(P("state", "node"), P("node", "state"), P("node", "state")),
        check_vma=False,
    )
```

```python
import functools

import jax
import jax.numpy as jnp
from jax import lax
from jax.experimental import pallas as pl
from jax.experimental.pallas import tpu as pltpu
from jax.sharding import PartitionSpec as P

MESH = pl.DeviceIdType.MESH
BF = jnp.bfloat16
F32 = jnp.float32


def split(x):
    hi = x.astype(BF)
    return hi, (x - hi.astype(F32)).astype(BF)


def mul(a, b):
    return jnp.dot(a, b, preferred_element_type=F32)


def mul3(a, b):
    return mul(a[0], b[0]) + (mul(a[0], b[1]) + mul(a[1], b[0]))


def mul3_stacked(a, b):
    rows = a.shape[0]
    hi, lo = split(a)
    both = mul(jnp.concatenate([hi, lo], 0), b[0])
    return both[:rows] + (both[rows:] + mul(hi, b[1]))


def kernel(
    n_node, n_state,
    states, coeffs, cell_matrix, connect, face_list, node_mass,
    rot, hout, mout,
    xhi, xlo, part, rrecv, lrecv, rout, lout,
    cells, links, st, twice, thi, tlo, ahi, alo, wbuf, whi, wlo, ghost, gsend, wghost,
    tot, qbuf, pairs, qsum, qrecv,
    rs_send, rs_recv, ls_send, ls_recv, p_send, p_recv, q_send, q_recv, g_sem, w_sem,
):
    me = lax.axis_index("node")
    pos = lax.axis_index("state")
    core = lax.rem(me, 2)
    chip = lax.div(me, 2)
    partner = me + 1 - 2 * core
    nodes, width = states.shape
    ext = st.shape[0]
    count, npe = connect.shape
    face = ext - nodes
    chunks, group, _ = hout.shape
    pieces = part.shape[0]
    per = pieces // chunks
    rows = n_node * group
    chips = n_node // 2
    last = n_state - 1
    lag = 2
    steps = pieces + lag * last
    owned = rot.shape[0]
    x = (xhi.at[pl.ds(0, nodes)], xlo.at[pl.ds(0, nodes)])

    barrier = pltpu.get_barrier_semaphore()
    for k in range(1, n_node):
        pl.semaphore_signal(
            barrier, inc=1, device_id={"node": lax.rem(me + k, n_node)}, device_id_type=MESH
        )

    @pl.when(pos > 0)
    def _():
        pl.semaphore_signal(barrier, inc=1, device_id={"state": pos - 1}, device_id_type=MESH)

    @pl.when(pos < last)
    def _():
        pl.semaphore_signal(barrier, inc=1, device_id={"state": pos + 1}, device_id_type=MESH)

    hi, lo = split(states[...])
    x[0][...] = hi
    x[1][...] = lo
    value = mul3((hi, lo), split(coeffs[...])).T
    value = value.reshape(n_node, chunks, group, nodes)
    owners = n_node // per
    for t in range(chunks):
        for j in range(per):
            part[per * t + j] = value[owners * j:owners * (j + 1), t].reshape(owners * group, nodes)

    @pl.when(pos == 0)
    def _():
        rrecv[...] = jnp.zeros_like(rrecv)

    @pl.when(pos == last)
    def _():
        lrecv[...] = jnp.zeros_like(lrecv)

    @pl.when((pos > 0) & (pos < last))
    def _():
        pl.semaphore_wait(barrier, n_node + 1)

    @pl.when((pos == 0) | (pos == last))
    def _():
        pl.semaphore_wait(barrier, n_node)

    def ghost_copy(to):
        return pltpu.make_async_remote_copy(
            src_ref=gsend, dst_ref=ghost, send_sem=g_sem.at[0], recv_sem=g_sem.at[1],
            device_id={"node": to}, device_id_type=MESH,
        )

    def back_copy(to):
        return pltpu.make_async_remote_copy(
            src_ref=wbuf.at[pl.ds(nodes, face)], dst_ref=wghost, send_sem=w_sem.at[0], recv_sem=w_sem.at[1],
            device_id={"node": to}, device_id_type=MESH,
        )

    def right_copy(q):
        return pltpu.make_async_remote_copy(
            src_ref=rout.at[q], dst_ref=rrecv.at[q], send_sem=rs_send.at[q], recv_sem=rs_recv.at[q],
            device_id={"state": lax.rem(pos + 1, n_state)}, device_id_type=MESH,
        )

    def left_copy(q):
        return pltpu.make_async_remote_copy(
            src_ref=lout.at[q], dst_ref=lrecv.at[q], send_sem=ls_send.at[q], recv_sem=ls_recv.at[q],
            device_id={"state": lax.rem(pos + last, n_state)}, device_id_type=MESH,
        )

    def pair_copy(e):
        return pltpu.make_async_remote_copy(
            src_ref=qbuf.at[e, :, 1 - core], dst_ref=pairs.at[e],
            send_sem=p_send.at[e], recv_sem=p_recv.at[e],
            device_id={"node": partner}, device_id_type=MESH,
        )

    def panel_copy(e, k):
        to = lax.rem(chip + k, chips)
        return pltpu.make_async_remote_copy(
            src_ref=qsum.at[e, to], dst_ref=qrecv.at[e, k - 1],
            send_sem=q_send.at[e, k - 1], recv_sem=q_recv.at[e, k - 1],
            device_id={"node": 2 * to + core}, device_id_type=MESH,
        )

    def line_step(h):
        q = h - lag * pos

        @pl.when((q >= 0) & (q < pieces))
        def _():
            @pl.when(pos > 0)
            def _():
                right_copy(q).wait_recv()

            @pl.when(pos < last)
            def _():
                rout[q] = part[q] + rrecv[q]
                right_copy(q).start()

        g = h - lag * (last - pos)

        @pl.when((g >= 0) & (g < pieces))
        def _():
            @pl.when(pos < last)
            def _():
                left_copy(g).wait_recv()

            @pl.when(pos > 0)
            def _():
                lout[g] = part[g] + lrecv[g]
                left_copy(g).start()

    def line_steps(begin, end):
        @pl.loop(begin, end)
        def _(h):
            line_step(h)

    for done in range(lag):
        line_step(done)
    face_t = (
        lax.broadcasted_iota(jnp.int32, (nodes, face), 0) == face_list[...].reshape(1, face)
    ).astype(F32)
    face_cols = face_t.astype(BF)
    face_rows = face_t.T.astype(BF)
    gsend[...] = mul(face_rows, x[0][...]) + mul(face_rows, x[1][...])

    @pl.when(me > 0)
    def _():
        ghost_copy(lax.rem(me + n_node - 1, n_node)).start()

    line_step(lag)
    cells[...] = jnp.zeros_like(cells)
    cells[:, :npe, :npe] = cell_matrix[...]
    links[...] = jnp.full(links.shape, -1, jnp.int32)
    links[:count, :npe] = connect[...]
    columns = links[...].T
    done = lag + 1
    for c in range(count):
        st[:, 128 * c:128 * (c + 1)] = (
            lax.broadcasted_iota(jnp.int32, (ext, 128), 0) == links[c:c + 1]
        ).astype(F32).astype(BF)
        pick = (
            lax.broadcasted_iota(jnp.int32, (128, ext), 1) == columns[:, c:c + 1]
        ).astype(F32).astype(BF)
        twice[pl.ds(0, 128)] = pick
        twice[pl.ds(128, 128)] = pick
        cell = cells[c]
        t_hi, t_lo = split(mul(jnp.concatenate(split(0.5 * (cell + cell.T)), 1), twice[...]))
        thi[pl.ds(128 * c, 128)] = t_hi
        tlo[pl.ds(128 * c, 128)] = t_lo
        if c % 6 == 5:
            line_step(done)
            done += 1
    for begin in range(0, ext - 128, 256):
        end = begin + 256 if ext - begin - 256 >= 128 else ext
        a_hi, a_lo = split(mul(st[...], thi[:, begin:end]) + mul(st[...], tlo[:, begin:end]))
        ahi[:, begin:end] = a_hi
        alo[:, begin:end] = a_lo
        line_step(done)
        done += 1

    @pl.when(me < n_node - 1)
    def _():
        ghost_copy(lax.rem(me + 1, n_node)).wait_recv()

    @pl.when(me == n_node - 1)
    def _():
        ghost[...] = jnp.zeros_like(ghost)

    g_hi, g_lo = split(ghost[...])
    xhi[pl.ds(nodes, face)] = g_hi
    xlo[pl.ds(nodes, face)] = g_lo

    at = pl.ds(nodes, face)
    wbuf[at] = mul3((ahi[at], alo[at]), (xhi[...], xlo[...]))

    @pl.when(me < n_node - 1)
    def _():
        back_copy(lax.rem(me + 1, n_node)).start()

    at = pl.ds(0, nodes)
    for begin in range(0, width, 256):
        cols = slice(begin, begin + 256)
        wbuf[at, cols] = mul3((ahi[at], alo[at]), (xhi[:, cols], xlo[:, cols]))
        line_step(done)
        done += 1

    @pl.when(me > 0)
    def _():
        back_copy(lax.rem(me + n_node - 1, n_node)).wait_recv()

    @pl.when(me == 0)
    def _():
        wghost[...] = jnp.zeros_like(wghost)

    b_hi, b_lo = split(wghost[...])
    w_hi, w_lo = split(wbuf[pl.ds(0, nodes)] + mul(face_cols, b_hi) + mul(face_cols, b_lo))
    whi[...] = w_hi
    wlo[...] = w_lo

    def ready(t):
        return jnp.minimum(jnp.maximum(done + 2 * t, per * (t + 1) + lag * last), steps)

    def finish(t):
        for i, out in enumerate((hout, mout)):
            value = qsum[2 * t + i, chip]
            for k in range(1, chips):
                panel_copy(2 * t + i, k).wait_recv()
                value = value + qrecv[2 * t + i, k - 1]
            out[t] = value

    def pass_on(e):
        pair_copy(e).wait_recv()
        qsum[e] = qbuf[e, :, core] + pairs[e]
        for k in range(1, chips):
            panel_copy(e, k).start()

    line_steps(done, ready(0))

    def body(t, carry):
        begin, end = ready(t), ready(t + 1)
        middle = jnp.minimum(begin + 1, end)
        every = pl.ds(per * t, per)
        total = (part[every] + rrecv[every] + lrecv[every]).reshape(rows, nodes)
        tot[...] = total.reshape(n_node, group, nodes)
        rot[:, t] = tot[pl.ds(pos * owned, owned)]
        qbuf[2 * t] = mul3_stacked(total, (whi[...], wlo[...])).reshape(chips, 2, group, width)
        pair_copy(2 * t).start()

        @pl.when(t > 0)
        def _():
            pass_on(2 * t - 1)

        line_steps(begin, middle)
        total = tot[...].reshape(rows, nodes) * node_mass[...].reshape(1, nodes)
        qbuf[2 * t + 1] = mul3_stacked(total, (x[0][...], x[1][...])).reshape(chips, 2, group, width)
        pair_copy(2 * t + 1).start()
        pass_on(2 * t)
        line_steps(middle, end)

        @pl.when(t > 1)
        def _():
            finish(t - 2)

        return carry

    lax.fori_loop(0, chunks, body, 0)
    pass_on(2 * chunks - 1)
    if chunks > 1:
        finish(chunks - 2)
    finish(chunks - 1)

    @pl.when(me > 0)
    def _():
        ghost_copy(lax.rem(me + n_node - 1, n_node)).wait_send()

    @pl.when(me < n_node - 1)
    def _():
        back_copy(lax.rem(me + 1, n_node)).wait_send()

    @pl.loop(0, pieces)
    def _(q):
        @pl.when(pos < last)
        def _():
            right_copy(q).wait_send()

        @pl.when(pos > 0)
        def _():
            left_copy(q).wait_send()

    @pl.loop(0, 2 * chunks)
    def _(e):
        pair_copy(e).wait_send()
        for k in range(1, chips):
            panel_copy(e, k).wait_send()


def deliver(a, b, c, a_out, b_out, c_out):
    a_out[...] = a[...]
    b_out[...] = b[...]
    c_out[...] = c[...]


def local(n_node, n_state, states, coeffs, cell_matrix, connect, face_list, node_mass):
    nodes, width = states.shape
    block = coeffs.shape[1]
    count = connect.shape[0]
    face = face_list.shape[0]
    ext = nodes + face
    group = 16
    chunks = block // n_node // group
    pieces = 2 * chunks
    chips = n_node // 2
    owned = n_node // n_state
    vmem = pl.BlockSpec(memory_space=pltpu.VMEM)
    line = pltpu.VMEM((pieces, n_node * group // 2, nodes), F32)
    outs = pl.pallas_call(
        functools.partial(kernel, n_node, n_state),
        out_shape=(
            jax.ShapeDtypeStruct((owned, chunks, group, nodes), F32),
            jax.ShapeDtypeStruct((chunks, group, width), F32),
            jax.ShapeDtypeStruct((chunks, group, width), F32),
        ),
        in_specs=[vmem] * 6,
        out_specs=(vmem,) * 3,
        scratch_shapes=[
            pltpu.VMEM((ext, width), BF),
            pltpu.VMEM((ext, width), BF),
            line, line, line, line, line,
            pltpu.VMEM((count, 128, 128), F32),
            pltpu.VMEM((-(-count // 8) * 8, 128), jnp.int32),
            pltpu.VMEM((ext, count * 128), BF),
            pltpu.VMEM((256, ext), BF),
            pltpu.VMEM((count * 128, ext), BF),
            pltpu.VMEM((count * 128, ext), BF),
            pltpu.VMEM((ext, ext), BF),
            pltpu.VMEM((ext, ext), BF),
            pltpu.VMEM((ext, width), F32),
            pltpu.VMEM((nodes, width), BF),
            pltpu.VMEM((nodes, width), BF),
            pltpu.VMEM((face, width), F32),
            pltpu.VMEM((face, width), F32),
            pltpu.VMEM((face, width), F32),
            pltpu.VMEM((n_node, group, nodes), F32),
            pltpu.VMEM((2 * chunks, chips, 2, group, width), F32),
            pltpu.VMEM((2 * chunks, chips, group, width), F32),
            pltpu.VMEM((2 * chunks, chips, group, width), F32),
            pltpu.VMEM((2 * chunks, chips - 1, group, width), F32),
            pltpu.SemaphoreType.DMA((pieces,)),
            pltpu.SemaphoreType.DMA((pieces,)),
            pltpu.SemaphoreType.DMA((pieces,)),
            pltpu.SemaphoreType.DMA((pieces,)),
            pltpu.SemaphoreType.DMA((2 * chunks,)),
            pltpu.SemaphoreType.DMA((2 * chunks,)),
            pltpu.SemaphoreType.DMA((2 * chunks, chips - 1)),
            pltpu.SemaphoreType.DMA((2 * chunks, chips - 1)),
            pltpu.SemaphoreType.DMA((2,)),
            pltpu.SemaphoreType.DMA((2,)),
        ],
        compiler_params=pltpu.CompilerParams(
            collective_id=0, has_side_effects=True, vmem_limit_bytes=60 * 1024 * 1024
        ),
    )(states, coeffs, cell_matrix, connect, face_list, node_mass)
    shapes = ((block // n_state, nodes), (block // n_node, width), (block // n_node, width))
    return pl.pallas_call(
        deliver,
        out_shape=tuple(jax.ShapeDtypeStruct(shape, F32) for shape in shapes),
        in_specs=[vmem] * 3,
        out_specs=(vmem,) * 3,
        compiler_params=pltpu.CompilerParams(vmem_limit_bytes=60 * 1024 * 1024),
    )(*(out.reshape(shape) for out, shape in zip(outs, shapes)))


def solution(mesh):
    return jax.shard_map(
        functools.partial(local, mesh.shape["node"], mesh.shape["state"]),
        mesh=mesh,
        in_specs=(
            P("node", "state"),
            P("state", None),
            P("node", None, None),
            P("node", None),
            P("node"),
            P("node"),
        ),
        out_specs=(P("state", "node"), P("node", "state"), P("node", "state")),
        check_vma=False,
    )
```
